512 devices in a mesh: cls: 16 (over z, core), dir: 32 (over y, x).
Axes of the slice: x: 4, y: 8, z: 8, core: 2. Of those that a mesh axis runs over, the one named last changes fastest.
Arguments:
- particles: bfloat16 [256, 4224], P('cls', 'dir')
- assignments: int32 [256, 1], P('cls'), may hold values from 0 to 15; in each aligned block of 16 rows (0 to 15, 16 to 31, ...) at most 3 rows name the same one
- defocus_bins: int32 [256], P('cls'), may hold values from 0 to 63
- ctf_table: float32 [64, 33], replicated, may hold values from -1 to 1
- references: bfloat16 [16, 4608, 4224], P('cls', 'dir'), may hold values from -6 to 6
Outputs:
- best_score: float32 [256], P('cls')
- normalized: float32 [256], P('cls')
The draws below stay inside these ranges and needn't reach their ends.
Inputs may be any that keep to these rules, and one draw needn't show every extreme that they name: `assignments`: among the 16 particles of one index of cls no class is named more than 3 times; one class is named exactly 3 times in some of them.
All inputs are finite; a program needn't handle non-finite values.
Results may differ from the reference program's by a relative error of at most 0.0017.
Values may be sent and summed in bfloat16 or wider, within the bound.
A program may use at most 64 MiB of HBM per device.

```python
import math
import jax
import jax.numpy as jnp
import numpy as np
from jax import lax

CYCLES = 33
ANGLES = 64
ROTS = 16
BINS = 64
PART_ROW = 16
FEAT = 4224
DIRS = 4608
CLASSES = 16
CAP = 3
SLOTS = 48
PARTICLES = 256


def draw_particles(key, part):
    key = jax.random.fold_in(key, 11)
    key_scale, key_base = jax.random.split(key)
    row_count = PARTICLES // PART_ROW
    row_index = (jnp.arange(PARTICLES, dtype=jnp.int32) // PART_ROW).astype(jnp.float32)
    jitter = jax.random.uniform(key_scale, (PARTICLES,), jnp.float32)
    scales = 10.0 ** ((row_index + jitter) / row_count)
    base = jax.random.normal(key_base, (PARTICLES, FEAT), jnp.float32)
    return (scales[:, None] * base).astype(jnp.bfloat16)


def place_ends(values, rng, least, largest):
    index_at = [jax.random.randint(jax.random.fold_in(rng, axis), (), 0, length) for axis, length in enumerate(values.shape)]
    main_axis = values.shape.index(max(values.shape))
    next_to = index_at[:main_axis] + [(index_at[main_axis] + 1) % values.shape[main_axis]] + index_at[main_axis + 1:]
    return values.at[tuple(index_at)].set(least).at[tuple(next_to)].set(largest)


def level_of(rng, shape, cuts, least, largest):
    def one(axis_at, parts):
        heights = jax.random.uniform(jax.random.fold_in(jax.random.fold_in(rng, 6), axis_at), (parts,), jnp.float32, least / len(cuts), largest / len(cuts))
        return jnp.repeat(jnp.exp(heights), shape[axis_at] // parts).reshape((-1,) + (1,) * (len(shape) - axis_at - 1))

    factor_of = one(*cuts[0])
    for cut in cuts[1:]:
        factor_of = factor_of * one(*cut)
    return factor_of


def assign_block(rng, own, number, rows, number_of, top, most, slope):
    sequence = jax.random.permutation(rng, number_of)
    crowded, common = load_shares(number_of, rows * top, most, slope, True), load_shares(number_of, rows * top, most, slope, False)
    places = jnp.arange(number_of)

    def named(sizes, offset_by):
        used = int((sizes > 0).sum())
        fixed = max(1, used // 4)
        passed = fixed + (places - fixed + offset_by * (used - fixed)) % max(1, number_of - fixed)
        return jnp.zeros((number_of,), jnp.int32).at[sequence[jnp.where(places < fixed, places, passed)]].set(jnp.asarray(sizes, jnp.int32))

    sizes = jnp.where(number % 4 == 0, named(crowded, number // 4), named(common, number - number // 4 - 1))
    mixed = jax.random.permutation(jax.random.fold_in(own, 3), number_of)
    giver, receiver = mixed[0:number_of // 2 * 2:2], mixed[1:number_of // 2 * 2:2]
    room = jnp.minimum(sizes[giver] - 1, most - sizes[receiver]) // 2
    room = jnp.where((giver == sequence[0]) | (receiver == sequence[0]) | (sizes[receiver] == 0), 0, jnp.maximum(room, 0))
    passed = jax.random.randint(jax.random.fold_in(own, 4), (number_of // 2,), 0, 1 << 20) % (room + 1)
    sizes = sizes.at[giver].add(-passed).at[receiver].add(passed)
    members = jnp.searchsorted(jnp.cumsum(sizes), jnp.arange(rows * top), side="right").astype(jnp.int32)
    table = members.reshape(top, rows).T
    table = table[jax.random.permutation(jax.random.fold_in(own, 1), rows)]
    offset_by = jax.random.randint(jax.random.fold_in(own, 2), (rows, 1), 0, top)
    return jnp.take_along_axis(table, (jnp.arange(top)[None, :] + offset_by) % top, axis=1)


def load_shares(amount, total, limit, slope, full):
    loads = [(1 << 20) // math.isqrt(standing ** slope) + 1 for standing in range(1, amount + 1)]
    largest = limit if full else min(limit, max(-(-total // amount), total * loads[0] // sum(loads)))
    least = 1 if total - largest >= amount - 1 else 0
    holding, surplus = [largest] + [least] * (amount - 1), total - largest - least * (amount - 1)
    while surplus > 0:
        movable = [i for i in range(1, amount) if holding[i] < largest] or [i for i in range(1, amount) if holding[i] < limit]
        pool, remaining = sum([loads[i] for i in movable]), surplus
        for i in movable:
            extra = min(limit - holding[i], max(1, remaining * loads[i] // pool), surplus)
            holding[i] = holding[i] + extra
            surplus = surplus - extra
    return np.array(holding)


def centred(own_key, shape, width, reach, pieces=(), held_as=jnp.bfloat16):
    gain = level_of(own_key, shape, pieces, -0.22, 0.18) if pieces else 1.0
    result = jax.random.normal(own_key, shape, jnp.float32) * width * gain
    return jnp.minimum(jnp.maximum(result, -reach), reach).astype(held_as)


def setup_inputs(seed: int = 0) -> dict:
    key_list = jax.random.split(jax.random.key(seed), 6)
    particles = draw_particles(jax.random.fold_in(key_list[5], 71), 0)
    assignments_keys = jax.random.split(jax.random.fold_in(key_list[1], 1), PARTICLES // PART_ROW)
    assignments_turns = jax.random.permutation(jax.random.fold_in(key_list[1], 3), PARTICLES // PART_ROW)
    assignments = jax.vmap(lambda own, number: assign_block(jax.random.fold_in(key_list[1], 2), own, number, PART_ROW, CLASSES, 1, CAP, 2))(assignments_keys, assignments_turns).reshape((PARTICLES, 1))
    defocus_bins = place_ends(jax.random.randint(key_list[2], (PARTICLES,), 0, BINS), jax.random.fold_in(key_list[2], 1), 0, BINS - 1).astype(jnp.int32)
    ctf_table = jnp.clip(jax.random.uniform(key_list[3], (BINS, CYCLES), jnp.float32, -1.0, 1.0), -1.0, 1.0)
    references = centred(key_list[4], (CLASSES, DIRS, FEAT), 1.0, 6.0, ((0, 16), (1, 32)))
    return {"particles": particles, "assignments": assignments, "defocus_bins": defocus_bins, "ctf_table": ctf_table, "references": references}


def reference(particles, assignments, defocus_bins, ctf_table, references):
    total_rows = particles.shape[0]
    assign = assignments[:, 0]
    onehot = (assign[:, None] == jnp.arange(CLASSES, dtype=jnp.int32)[None, :]).astype(jnp.int32)
    placing = lax.optimization_barrier(jnp.sum((jnp.cumsum(onehot, axis=0) - onehot) * onehot, axis=1))
    ctf_rows = ctf_table[defocus_bins]
    weighted = (particles.reshape(total_rows, CYCLES, 2 * ANGLES).astype(jnp.float32) * ctf_rows[:, :, None]).astype(jnp.bfloat16)
    weighted = weighted.reshape(total_rows, FEAT)
    scale = 1.0 / math.sqrt(FEAT / 3.0)
    stride = ANGLES // ROTS

    def per_class(carry, inputs):
        class_index, templates = inputs
        chosen = assign == class_index
        dispatch = ((placing[None, :] == jnp.arange(SLOTS, dtype=jnp.int32)[:, None]) & chosen[None, :]).astype(jnp.float32)
        picked = jnp.dot(dispatch.astype(jnp.bfloat16), weighted, preferred_element_type=jnp.float32).astype(jnp.bfloat16)
        ctf_picked = jnp.dot(dispatch, ctf_rows, precision=lax.Precision.HIGHEST)
        wide = templates.reshape(DIRS, CYCLES, 2 * ANGLES).astype(jnp.float32)
        energy = jnp.einsum('dra,dra->dr', wide, wide)
        penalty = 0.5 * jnp.dot(ctf_picked * ctf_picked, energy.T, precision=lax.Precision.HIGHEST)
        shaped = picked.reshape(SLOTS, CYCLES, ANGLES, 2)
        best = None
        for rotation in range(ROTS):
            turned = jnp.roll(shaped, rotation * stride, axis=2).reshape(SLOTS, FEAT)
            cross = jnp.dot(templates, turned.T, preferred_element_type=jnp.float32)
            value = lax.optimization_barrier(jnp.max((cross - penalty.T) * scale, axis=0))
            best = value if rotation == 0 else jnp.maximum(best, value)
        return (carry + jnp.dot(dispatch.T, best, precision=lax.Precision.HIGHEST), None)
    best_score, _ = lax.scan(per_class, jnp.zeros((total_rows,), jnp.float32), (jnp.arange(CLASSES, dtype=jnp.int32), references))
    spread = jnp.sum(best_score * best_score)
    normalized = best_score / jnp.sqrt(spread / total_rows + 1e-05)
    return (best_score, normalized)
```

```python
import math

import jax
import jax.numpy as jnp
from jax import lax
from jax.experimental import pallas as pl
from jax.experimental.pallas import tpu as pltpu
from jax.sharding import PartitionSpec as P

CYCLES = 33
ANGLES = 64
ROTS = 16
WIDE = 2 * ANGLES
FEAT = CYCLES * WIDE
STEP = 2 * (ANGLES // ROTS)
SCALE = 1.0 / math.sqrt(FEAT / 3.0)
NCLS = 16
NX = 4
NY = 8
NDIR = NX * NY
ROWS = 16
CAP = 3
SLOTS = NCLS * CAP
BINS = 64
TOTAL = 256
MESH = pl.DeviceIdType.MESH
HIGH = lax.Precision.HIGHEST
F32 = jnp.float32
BF16 = jnp.bfloat16
I32 = jnp.int32
HOPS = {1: (0, 1), 7: (0, 7), 2: (1, 0), 6: (3, 0), 3: (1, 1), 5: (3, 7), 4: (2, 0)}
ORDER = (1, 7, 2, 6, 3, 5, 4)


def iota(shape, dim):
    return lax.broadcasted_iota(I32, shape, dim)


def to_column(row, n):
    keep = iota((n, n), 0) == iota((n, n), 1)
    return jnp.sum(jnp.where(keep, jnp.broadcast_to(row, (n, n)), 0), axis=1, keepdims=True)


def to_row(column, n, lanes):
    keep = iota((n, lanes), 0) == iota((n, lanes), 1)
    return jnp.sum(
        jnp.where(keep, jnp.broadcast_to(column, (n, lanes)), 0), axis=0, keepdims=True
    )


def kernel(
    part_ref, assign_ref, bins_ref, table_ref, refs_ref, best_ref, norm_ref,
    tbuf, tset, tlast, energy, send0, send1, a0, a1, stack, bsend, brecv,
    gmain, gext, lhs, acc, dsend, dbuf, esend, ebuf,
    load_sem, a_send, a_recv, b_send, b_recv, c_send, c_recv, x_send, x_recv,
    d_send, d_recv, e_send, e_recv,
):
    me_c = lax.axis_index("cls")
    me_d = lax.axis_index("dir")
    x = lax.rem(me_d, NX)
    y = lax.div(me_d, NX)
    s = lax.rem(2 * x + y, 8)

    load = pltpu.make_async_copy(refs_ref.at[0], tbuf, load_sem)
    load.start()

    barrier = pltpu.get_barrier_semaphore()
    for d in range(1, NDIR):
        pl.semaphore_signal(
            barrier, inc=1, device_id=(me_c, lax.rem(me_d + d, NDIR)), device_id_type=MESH
        )
    for d in range(1, NCLS):
        pl.semaphore_signal(
            barrier, inc=1, device_id=(lax.rem(me_c + d, NCLS), me_d), device_id_type=MESH
        )

    assign_row = assign_ref[...]
    assign = to_column(assign_row, ROWS)
    bins = to_column(bins_ref[...], ROWS)
    same = (assign == jnp.broadcast_to(assign_row, (ROWS, ROWS))) & (
        iota((ROWS, ROWS), 1) < iota((ROWS, ROWS), 0)
    )
    placing = jnp.sum(same.astype(I32), axis=1, keepdims=True)
    slot = assign * CAP + placing

    onehot = bins == iota((ROWS, BINS), 1)
    row_a = table_ref[pl.ds(me_d, 1), :]
    row_b = table_ref[pl.ds(me_d + 1, 1), :]
    ctf_a = jnp.sum(jnp.where(onehot, row_a, 0.0), axis=1, keepdims=True)
    ctf_b = jnp.sum(jnp.where(onehot, row_b, 0.0), axis=1, keepdims=True)
    raw = jnp.concatenate(
        [part_ref[...].astype(F32), jnp.zeros((ROWS, 2 * WIDE - FEAT // NDIR), F32)], axis=1
    )
    raw = pltpu.roll(raw, 4 * me_d, 1)
    tile0 = (raw[:, :WIDE] * ctf_a).astype(BF16)
    tile1 = (raw[:, WIDE:] * ctf_b).astype(BF16)
    send0[...] = tile0
    send1[...] = tile1
    a0[x] = tile0

    lane = iota((ROWS, NCLS * ROWS), 1)
    to_class = lane // ROWS
    at_row = lane - to_class * ROWS
    third = (at_row * 171) >> 9
    hit = slot == to_class * CAP + at_row - third * CAP
    pieces = [(hit & (third == c)).astype(F32) for c in range(5)]
    pieces.append(((assign == to_class) & (at_row == ROWS - 1)).astype(F32))
    pieces.append(jnp.zeros((2 * ROWS, NCLS * ROWS), F32))
    packing = jnp.concatenate(pieces, axis=0).T.astype(BF16)
    aux = jnp.where(placing == iota((ROWS, WIDE), 1), (bins + 1).astype(F32), 0.0)
    stack[5 * ROWS : 6 * ROWS] = aux.astype(BF16)
    stack[6 * ROWS :] = jnp.zeros((2 * ROWS, WIDE), BF16)

    pl.semaphore_wait(barrier, NDIR + NCLS - 2)

    for d in range(1, NX):
        c = lax.rem(x + d, NX)
        to = lax.rem(s + 16 - 2 * c, NY) * NX + c
        pltpu.make_async_remote_copy(
            src_ref=send0, dst_ref=a0.at[x], send_sem=a_send, recv_sem=a_recv,
            device_id=(me_c, to), device_id_type=MESH,
        ).start()
    next_x = lax.rem(x + 1, NX)
    next_y = lax.rem(lax.div(me_d + 1, NX), NY)
    next_s = lax.rem(2 * next_x + next_y, 8)
    for c in range(NX):
        to = lax.rem(next_s + 16 - 2 * c, NY) * NX + c
        pltpu.make_async_remote_copy(
            src_ref=send1, dst_ref=a1.at[next_x], send_sem=a_send, recv_sem=a_recv,
            device_id=(me_c, to), device_id_type=MESH,
        ).start()

    q = iota((SLOTS, TOTAL), 0)
    sender = (q * 171) >> 9
    source = sender * ROWS + q - sender * CAP
    column = iota((SLOTS, TOTAL), 1)
    unpack = jnp.concatenate(
        [(column == source + c * CAP).astype(F32) for c in range(5)]
        + [(column == sender * ROWS + ROWS - 1).astype(F32)],
        axis=0,
    ).astype(BF16)

    a_all = stack.at[pl.ds(0, 7 * ROWS)]
    pltpu.make_async_copy(a_all, a_all, a_recv).wait()
    first = (s != 0).astype(F32)
    for c in range(NX):
        late = a1[c].astype(F32)
        if c == 0:
            stack[4 * ROWS : 5 * ROWS] = (late * (1.0 - first)).astype(BF16)
            late = late * first
        stack[c * ROWS : (c + 1) * ROWS] = (a0[c].astype(F32) + late).astype(BF16)

    packed = jnp.dot(packing, stack[...], preferred_element_type=F32)
    bsend[...] = packed.astype(BF16)
    mine = pl.ds(pl.multiple_of(me_c * ROWS, ROWS), ROWS)
    for d in range(1, NCLS):
        to = lax.rem(me_c + d, NCLS)
        pltpu.make_async_remote_copy(
            src_ref=bsend.at[pl.ds(pl.multiple_of(to * ROWS, ROWS), ROWS)],
            dst_ref=brecv.at[mine], send_sem=b_send, recv_sem=b_recv,
            device_id=(to, me_d), device_id_type=MESH,
        ).start()
    brecv[mine] = bsend[mine]

    load.wait()
    for c in range(NX):
        for z in range(8):
            j = ((z + 8 - 2 * c) % 8) * NX + c
            tset[z, :, c * WIDE : (c + 1) * WIDE] = tbuf[:, j * WIDE : (j + 1) * WIDE]
    tlast[...] = tbuf[:, (CYCLES - 1) * WIDE :]

    b_all = brecv.at[pl.ds(0, (NCLS - 1) * ROWS)]
    pltpu.make_async_copy(b_all, b_all, b_recv).wait()
    unpacked = jnp.dot(unpack, brecv[...], preferred_element_type=F32)
    gmain[0] = unpacked[: 4 * SLOTS].astype(BF16)

    @pl.when(s == 0)
    def _():
        gext[...] = unpacked[4 * SLOTS : 5 * SLOTS].astype(BF16)

    for d in ORDER:
        dx, dy = HOPS[d]
        to = lax.rem(y + dy, NY) * NX + lax.rem(x + dx, NX)
        pltpu.make_async_remote_copy(
            src_ref=gmain.at[0], dst_ref=gmain.at[d], send_sem=c_send, recv_sem=c_recv.at[d],
            device_id=(me_c, to), device_id_type=MESH,
        ).start()

    @pl.when(s == 0)
    def _():
        for d in ORDER:
            dx, dy = HOPS[d]
            to = lax.rem(y + dy, NY) * NX + lax.rem(x + dx, NX)
            pltpu.make_async_remote_copy(
                src_ref=gext, dst_ref=gext, send_sem=x_send, recv_sem=x_recv,
                device_id=(me_c, to), device_id_type=MESH,
            ).start()

    lanes = iota((1, WIDE), 1)
    total = jnp.zeros((tbuf.shape[0], WIDE), F32)
    for k in range(CYCLES):
        block = tbuf[:, k * WIDE : (k + 1) * WIDE].astype(F32)
        total = jnp.where(lanes == k, jnp.sum(block * block, axis=1, keepdims=True), total)
    energy[...] = total
    third_lane = iota((SLOTS, WIDE), 0) - 3 * ((iota((SLOTS, WIDE), 0) * 171) >> 9)
    got = jnp.sum(
        jnp.where(iota((SLOTS, WIDE), 1) == third_lane, unpacked[5 * SLOTS :], 0.0),
        axis=1, keepdims=True,
    ).astype(I32)
    bin_hot = (got == iota((SLOTS, BINS), 1) + 1).astype(F32)
    table = table_ref[...]
    table = jnp.concatenate([table, jnp.zeros((WIDE - CYCLES, BINS), F32)], axis=0)
    nt = (((1,), (1,)), ((), ()))
    ctf = lax.dot_general(bin_hot, table, nt, precision=HIGH, preferred_element_type=F32)
    penalty = 0.5 * lax.dot_general(
        ctf * ctf, energy[...], nt, precision=HIGH, preferred_element_type=F32
    )

    def turn(block, at):
        for r in range(ROTS):
            lhs[r * SLOTS : (r + 1) * SLOTS, at * WIDE : (at + 1) * WIDE] = pltpu.roll(
                block, r * STEP, 1
            )

    def add_set(d):
        for c in range(NX):
            turn(gmain[d, c * SLOTS : (c + 1) * SLOTS, :], c)
        term = lax.dot_general(
            lhs[...], tset[lax.rem(s + 8 - d, 8)], nt, preferred_element_type=F32
        )
        if d == 0:
            acc[...] = term
        else:
            acc[...] += term

    add_set(0)
    for d in ORDER:
        pltpu.make_async_copy(gmain.at[d], gmain.at[d], c_recv.at[d]).wait()
        add_set(d)

    @pl.when(s != 0)
    def _():
        pltpu.make_async_copy(gext, gext, x_recv).wait()

    turn(gext[...], 0)
    cross = acc[...] + lax.dot_general(
        lhs[:, :WIDE], tlast[...], nt, preferred_element_type=F32
    )
    top = cross[:SLOTS]
    for r in range(1, ROTS):
        top = jnp.maximum(top, cross[r * SLOTS : (r + 1) * SLOTS])
    local = jnp.max((top - penalty) * SCALE, axis=1, keepdims=True)
    local = to_row(local, SLOTS, WIDE)

    dsend[...] = local
    dbuf[me_d] = local
    for d in range(1, NDIR):
        pltpu.make_async_remote_copy(
            src_ref=dsend, dst_ref=dbuf.at[me_d], send_sem=d_send, recv_sem=d_recv,
            device_id=(me_c, lax.rem(me_d + d, NDIR)), device_id_type=MESH,
        ).start()
    d_all = dbuf.at[pl.ds(0, NDIR - 1)]
    pltpu.make_async_copy(d_all, d_all, d_recv).wait()
    group = jnp.max(dbuf[...], axis=0)

    squares = jnp.sum(group * group, axis=1, keepdims=True)
    answer = jnp.where(lanes == SLOTS, squares, group)
    esend[...] = answer
    ebuf[me_c] = answer
    for d in range(1, NCLS):
        pltpu.make_async_remote_copy(
            src_ref=esend, dst_ref=ebuf.at[me_c], send_sem=e_send, recv_sem=e_recv,
            device_id=(lax.rem(me_c + d, NCLS), me_d), device_id_type=MESH,
        ).start()
    e_all = ebuf.at[pl.ds(0, NCLS - 1)]
    pltpu.make_async_copy(e_all, e_all, e_recv).wait()

    spread = jnp.zeros((1, WIDE), F32)
    chosen = jnp.zeros((ROWS, WIDE), F32)
    for g in range(NCLS):
        spread = spread + ebuf[g]
        chosen = jnp.where(assign == g, ebuf[g], chosen)
    spread = jnp.sum(jnp.where(lanes == SLOTS, spread, 0.0), axis=1, keepdims=True)
    own = jnp.sum(
        jnp.where(iota((ROWS, WIDE), 1) == me_c * CAP + placing, chosen, 0.0),
        axis=1, keepdims=True,
    )
    own = to_row(own, ROWS, ROWS)
    best_ref[...] = own
    norm_ref[...] = own / jnp.sqrt(spread / TOTAL + 1e-05)

    a_all = stack.at[pl.ds(0, 7 * ROWS)]
    pltpu.make_async_copy(a_all, a_all, a_send).wait()
    pltpu.make_async_copy(b_all, b_all, b_send).wait()
    c_all = gmain.at[pl.ds(1, 7)]
    pltpu.make_async_copy(c_all, c_all, c_send).wait()

    @pl.when(s == 0)
    def _():
        x_all = lhs.at[pl.ds(0, 7 * SLOTS), pl.ds(0, WIDE)]
        pltpu.make_async_copy(x_all, x_all, x_send).wait()

    pltpu.make_async_copy(d_all, d_all, d_send).wait()
    pltpu.make_async_copy(e_all, e_all, e_send).wait()


def on_device(particles, assignments, defocus_bins, ctf_table, references):
    dirs = references.shape[1]
    vmem = pl.BlockSpec(memory_space=pltpu.VMEM)
    scratch = [
        pltpu.VMEM((dirs, FEAT), BF16),
        pltpu.VMEM((8, dirs, NX * WIDE), BF16),
        pltpu.VMEM((dirs, WIDE), BF16),
        pltpu.VMEM((dirs, WIDE), F32),
        pltpu.VMEM((ROWS, WIDE), BF16),
        pltpu.VMEM((ROWS, WIDE), BF16),
        pltpu.VMEM((NX, ROWS, WIDE), BF16),
        pltpu.VMEM((NX, ROWS, WIDE), BF16),
        pltpu.VMEM((8 * ROWS, WIDE), BF16),
        pltpu.VMEM((NCLS * ROWS, WIDE), BF16),
        pltpu.VMEM((NCLS * ROWS, WIDE), BF16),
        pltpu.VMEM((8, 4 * SLOTS, WIDE), BF16),
        pltpu.VMEM((SLOTS, WIDE), BF16),
        pltpu.VMEM((ROTS * SLOTS, NX * WIDE), BF16),
        pltpu.VMEM((ROTS * SLOTS, dirs), F32),
        pltpu.VMEM((1, WIDE), F32),
        pltpu.VMEM((NDIR, 1, WIDE), F32),
        pltpu.VMEM((1, WIDE), F32),
        pltpu.VMEM((NCLS, 1, WIDE), F32),
    ]
    dma = pltpu.SemaphoreType.DMA
    sems = [dma, dma, dma, dma, dma, dma, dma((8,)), dma, dma, dma, dma, dma, dma]
    best, norm = pl.pallas_call(
        kernel,
        out_shape=[jax.ShapeDtypeStruct((1, ROWS), F32)] * 2,
        in_specs=[vmem, vmem, vmem, vmem, pl.BlockSpec(memory_space=pl.ANY)],
        out_specs=[vmem, vmem],
        scratch_shapes=scratch + sems,
        compiler_params=pltpu.CompilerParams(
            collective_id=0, has_side_effects=True, vmem_limit_bytes=40 * 1024 * 1024
        ),
    )(
        particles,
        assignments.reshape(1, ROWS),
        defocus_bins.reshape(1, ROWS),
        ctf_table.T,
        references,
    )
    return best.reshape(ROWS), norm.reshape(ROWS)


def solution(mesh):
    placed = (P("cls", "dir"), P("cls", None), P("cls"), P(), P("cls", "dir", None))
    return jax.shard_map(
        on_device, mesh=mesh, in_specs=placed, out_specs=(P("cls"), P("cls")), check_vma=False
    )
```

```python
import math

import jax
import jax.numpy as jnp
from jax import lax
from jax.experimental import pallas as pl
from jax.experimental.pallas import tpu as pltpu
from jax.sharding import PartitionSpec as P

CYCLES = 33
ANGLES = 64
ROTS = 16
WIDE = 2 * ANGLES
FEAT = CYCLES * WIDE
STEP = 2 * (ANGLES // ROTS)
SCALE = 1.0 / math.sqrt(FEAT / 3.0)
NCLS = 16
NX = 4
NY = 8
NDIR = NX * NY
ROWS = 16
CAP = 3
SLOTS = NCLS * CAP
BINS = 64
TOTAL = 256
MESH = pl.DeviceIdType.MESH
HIGH = lax.Precision.HIGHEST
F32 = jnp.float32
BF16 = jnp.bfloat16
I32 = jnp.int32
LIMIT = 63 * 1024 * 1024


def iota(shape, dim):
    return lax.broadcasted_iota(I32, shape, dim)


def to_column(row, n):
    keep = iota((n, n), 0) == iota((n, n), 1)
    return jnp.sum(jnp.where(keep, jnp.broadcast_to(row, (n, n)), 0), axis=1, keepdims=True)


def to_row(column, n, lanes):
    keep = iota((n, lanes), 0) == iota((n, lanes), 1)
    return jnp.sum(
        jnp.where(keep, jnp.broadcast_to(column, (n, lanes)), 0), axis=0, keepdims=True
    )


def settle(ref, sem):
    pltpu.make_async_copy(ref, ref, sem).wait()


def kernel(
    part_hbm, assign_hbm, bins_hbm, table_hbm, refs_hbm, out_ref,
    part_ref, assign_ref, bins_ref, table_ref, tbuf, energy, bsend, brecv,
    grid, aux4, lhs, acc, dsend, dbuf, esend, ebuf,
    in_sem, load_sem, b_send, b_recv, y_send, y_recv, x_send, x_recv, u_send, u_recv,
    d_send, d_recv, e_send, e_recv,
):
    me_c = lax.axis_index("cls")
    me_d = lax.axis_index("dir")
    x = lax.rem(me_d, NX)
    y = lax.div(me_d, NX)

    barrier = pltpu.get_barrier_semaphore()
    peers = [(lax.rem(me_c + d, NCLS), me_d) for d in range(1, NCLS)]
    peers += [(me_c, lax.rem(y + d, NY) * NX + x) for d in range(1, NY)]
    peers += [(me_c, y * NX + lax.rem(x + d, NX)) for d in range(1, NX)]
    for peer in peers:
        pl.semaphore_signal(barrier, inc=1, device_id=peer, device_id_type=MESH)
    inputs = [
        pltpu.make_async_copy(source, target, in_sem.at[n])
        for n, (source, target) in enumerate(
            [
                (assign_hbm, assign_ref),
                (bins_hbm, bins_ref),
                (table_hbm, table_ref),
                (part_hbm, part_ref),
            ]
        )
    ]
    for copy in inputs:
        copy.start()
    load = pltpu.make_async_copy(refs_hbm.at[0], tbuf, load_sem)
    load.start()

    q = iota((4 * ROWS, TOTAL), 0)
    unpack = (iota((4 * ROWS, TOTAL), 1) == (q & 15) * ROWS + (q >> 4)).astype(F32).astype(BF16)
    for copy in inputs:
        copy.wait()

    assign_row = assign_ref[...]
    assign = to_column(assign_row, ROWS)
    bins = to_column(bins_ref[...], ROWS)
    same = (assign == jnp.broadcast_to(assign_row, (ROWS, ROWS))) & (
        iota((ROWS, ROWS), 1) < iota((ROWS, ROWS), 0)
    )
    placing = jnp.sum(same.astype(I32), axis=1, keepdims=True)

    lane = iota((ROWS, NCLS * ROWS), 1)
    at_row = lane & (ROWS - 1)
    named = assign == lane >> 4
    packing = jnp.concatenate(
        [
            (named & (at_row == placing)).astype(F32),
            (named & (at_row == CAP)).astype(F32),
            jnp.zeros((6 * ROWS, NCLS * ROWS), F32),
        ],
        axis=0,
    ).T.astype(BF16)

    onehot = bins == iota((ROWS, BINS), 1)
    row_a = table_ref[pl.ds(me_d, 1), :]
    row_b = table_ref[pl.ds(me_d + 1, 1), :]
    ctf_a = jnp.sum(jnp.where(onehot, row_a, 0.0), axis=1, keepdims=True)
    ctf_b = jnp.sum(jnp.where(onehot, row_b, 0.0), axis=1, keepdims=True)
    raw = part_ref[...].astype(F32)
    wide = iota((ROWS, WIDE), 1)
    main = raw[:, :WIDE]
    main = main * jnp.where(wide < WIDE - 4 * me_d, ctf_a, ctf_b)
    main = pltpu.roll(main, 4 * me_d, 1)
    left = jnp.concatenate([raw[:, WIDE:], jnp.zeros((ROWS, WIDE - 4), F32)], axis=1) * ctf_b
    aux = jnp.where(wide == 96 + placing, (bins + 1).astype(F32), 0.0)
    for t in range(CAP):
        aux = aux + jnp.where(placing == t, pltpu.roll(left, 12 * y + 4 * t, 1), 0.0)
    stack = jnp.concatenate([main, aux, jnp.zeros((6 * ROWS, WIDE), F32)], axis=0).astype(BF16)
    bsend[...] = jnp.dot(packing, stack, preferred_element_type=F32).astype(BF16)
    mine = pl.ds(pl.multiple_of(me_c * ROWS, ROWS), ROWS)
    brecv[mine] = bsend[mine]

    pl.semaphore_wait(barrier, len(peers))

    for d in (8, 9, 7, 10, 6, 11, 5, 12, 4, 13, 3, 14, 2, 15, 1):
        to = lax.rem(me_c + d, NCLS)
        pltpu.make_async_remote_copy(
            src_ref=bsend.at[pl.ds(pl.multiple_of(to * ROWS, ROWS), ROWS)],
            dst_ref=brecv.at[mine], send_sem=b_send, recv_sem=b_recv,
            device_id=(to, me_d), device_id_type=MESH,
        ).start()

    load.wait()
    lanes = iota((1, WIDE), 1)
    total = jnp.zeros((tbuf.shape[0], WIDE), F32)
    for k in range(CYCLES):
        block = tbuf[:, k * WIDE : (k + 1) * WIDE].astype(F32)
        total = jnp.where(lanes == k, jnp.sum(block * block, axis=1, keepdims=True), total)
    energy[...] = total

    b_all = brecv.at[pl.ds(0, (NCLS - 1) * ROWS)]
    settle(b_all, b_recv)
    unpacked = jnp.dot(unpack, brecv[...], preferred_element_type=F32)
    own = grid.at[y, x]
    own[...] = unpacked.astype(BF16)

    def forward(rho):
        row = lax.rem(y + rho, NY)
        block = grid.at[row, x, pl.ds(0, SLOTS)]
        for d in (2, 1, 3):
            pltpu.make_async_remote_copy(
                src_ref=block, dst_ref=block, send_sem=x_send, recv_sem=x_recv.at[d, rho],
                device_id=(me_c, y * NX + lax.rem(x + d, NX)), device_id_type=MESH,
            ).start()

    for d in (4, 3, 5, 2, 6, 1, 7):
        pltpu.make_async_remote_copy(
            src_ref=own, dst_ref=own, send_sem=y_send, recv_sem=y_recv.at[NY - d],
            device_id=(me_c, lax.rem(y + d, NY) * NX + x), device_id_type=MESH,
        ).start()
    forward(0)

    nt = (((1,), (1,)), ((), ()))
    got = jnp.concatenate(
        [unpacked[SLOTS:, 96 + t : 97 + t] for t in range(CAP)], axis=0
    ).astype(I32)
    bin_hot = (got == iota((SLOTS, BINS), 1) + 1).astype(F32)
    table = jnp.concatenate([table_ref[...], jnp.zeros((WIDE - CYCLES, BINS), F32)], axis=0)
    ctf = lax.dot_general(bin_hot, table, nt, precision=HIGH, preferred_element_type=F32)
    penalty = 0.5 * lax.dot_general(
        ctf * ctf, energy[...], nt, precision=HIGH, preferred_element_type=F32
    )

    for rho in (1, 7, 2, 6, 3, 5, 4):
        settle(grid.at[0, 0], y_recv.at[rho])
        forward(rho)
    over = jnp.zeros((ROWS, WIDE), F32)
    for row in range(NY):
        over = over + grid[row, x, SLOTS:, :].astype(F32)
    aux4[x] = over.astype(BF16)
    for d in (2, 1, 3):
        pltpu.make_async_remote_copy(
            src_ref=aux4.at[x], dst_ref=aux4.at[x], send_sem=u_send, recv_sem=u_recv,
            device_id=(me_c, y * NX + lax.rem(x + d, NX)), device_id_type=MESH,
        ).start()

    at = iota((1, CAP * WIDE), 1)
    place, at = at >> 7, at & (WIDE - 1)
    spread_to = ((at >> 2) & 3) * WIDE + (at >> 4) * 12 + place * 4 + (at & 3)
    spreading = (iota((NX * WIDE, CAP * WIDE), 0) == spread_to).astype(F32).astype(BF16)

    for rho in (0, 1, 7, 2, 6, 3, 5, 4):
        for d in range(1, NX):
            settle(grid.at[0, 0, pl.ds(0, SLOTS)], x_recv.at[d, rho])
    settle(aux4.at[pl.ds(0, 3)], u_recv)

    rest = jnp.concatenate([aux4[c] for c in range(NX)], axis=1)
    rest = jnp.dot(rest, spreading, preferred_element_type=F32).astype(BF16)
    rest = jnp.concatenate([rest[:, t * WIDE : (t + 1) * WIDE] for t in range(CAP)], axis=0)

    def turn(block, at):
        for r in range(ROTS):
            lhs[r * SLOTS : (r + 1) * SLOTS, at * WIDE : (at + 1) * WIDE] = pltpu.roll(
                block, r * STEP, 1
            )

    def select(low, high):
        return ((lanes >= low) & (lanes < high)).astype(F32).astype(BF16)

    def cycle(k):
        block = None
        if k < NDIR:
            block = grid[k // NX, k % NX, :SLOTS, :] * select(4 * k, WIDE)
        if k > 0:
            j = k - 1
            early = grid[j // NX, j % NX, :SLOTS, :] * select(0, 4 * j)
            early = early + rest * select(4 * j, 4 * k)
            block = early if block is None else block + early
        return block

    for row in range(NY):
        for c in range(NX):
            turn(cycle(row * NX + c), c)
        term = lax.dot_general(
            lhs[...], tbuf[:, row * NX * WIDE : (row + 1) * NX * WIDE], nt,
            preferred_element_type=F32,
        )
        if row == 0:
            acc[...] = term
        else:
            acc[...] += term
    turn(cycle(NDIR), 0)
    cross = acc[...] + lax.dot_general(
        lhs[:, :WIDE], tbuf[:, NDIR * WIDE :], nt, preferred_element_type=F32
    )
    top = cross[:SLOTS]
    for r in range(1, ROTS):
        top = jnp.maximum(top, cross[r * SLOTS : (r + 1) * SLOTS])
    local = jnp.max((top - penalty) * SCALE, axis=1, keepdims=True)
    local = to_row(local, SLOTS, WIDE)

    dsend[...] = local
    dbuf[me_d] = local
    far = sorted(range(1, NDIR), key=lambda d: -min(d // NX, NY - d // NX))
    for d in far:
        pltpu.make_async_remote_copy(
            src_ref=dsend, dst_ref=dbuf.at[me_d], send_sem=d_send, recv_sem=d_recv,
            device_id=(me_c, lax.rem(me_d + d, NDIR)), device_id_type=MESH,
        ).start()
    d_all = dbuf.at[pl.ds(0, NDIR - 1)]
    settle(d_all, d_recv)
    group = jnp.max(dbuf[...], axis=0)

    squares = jnp.sum(group * group, axis=1, keepdims=True)
    answer = jnp.where(lanes == SLOTS, squares, group)
    esend[...] = answer
    ebuf[me_c] = answer
    for d in (8, 9, 7, 10, 6, 11, 5, 12, 4, 13, 3, 14, 2, 15, 1):
        pltpu.make_async_remote_copy(
            src_ref=esend, dst_ref=ebuf.at[me_c], send_sem=e_send, recv_sem=e_recv,
            device_id=(lax.rem(me_c + d, NCLS), me_d), device_id_type=MESH,
        ).start()
    settle(b_all, b_send)
    settle(grid.at[pl.ds(0, 7), 0], y_send)
    settle(grid.at[pl.ds(0, NY), pl.ds(0, 3), pl.ds(0, SLOTS)], x_send)
    settle(aux4.at[pl.ds(0, 3)], u_send)
    settle(d_all, d_send)

    e_all = ebuf.at[pl.ds(0, NCLS - 1)]
    settle(e_all, e_recv)
    spread = jnp.zeros((1, WIDE), F32)
    chosen = jnp.zeros((ROWS, WIDE), F32)
    for g in range(NCLS):
        spread = spread + ebuf[g]
        chosen = jnp.where(assign == g, ebuf[g], chosen)
    spread = jnp.sum(jnp.where(lanes == SLOTS, spread, 0.0), axis=1, keepdims=True)
    best = jnp.sum(
        jnp.where(wide == placing * ROWS + me_c, chosen, 0.0), axis=1, keepdims=True
    )
    best = to_row(best, ROWS, ROWS)
    out_ref[0:1, :] = best
    out_ref[1:2, :] = best / jnp.sqrt(spread / TOTAL + 1e-05)
    settle(e_all, e_send)


def on_device(particles, assignments, defocus_bins, ctf_table, references):
    dirs = references.shape[1]
    vmem = pl.BlockSpec(memory_space=pltpu.VMEM)
    scratch = [
        pltpu.VMEM((ROWS, FEAT // NDIR), BF16),
        pltpu.VMEM((1, ROWS), I32),
        pltpu.VMEM((1, ROWS), I32),
        pltpu.VMEM((CYCLES, BINS), F32),
        pltpu.VMEM((dirs, FEAT), BF16),
        pltpu.VMEM((dirs, WIDE), F32),
        pltpu.VMEM((NCLS * ROWS, WIDE), BF16),
        pltpu.VMEM((NCLS * ROWS, WIDE), BF16),
        pltpu.VMEM((NY, NX, 4 * ROWS, WIDE), BF16),
        pltpu.VMEM((NX, ROWS, WIDE), BF16),
        pltpu.VMEM((ROTS * SLOTS, NX * WIDE), BF16),
        pltpu.VMEM((ROTS * SLOTS, dirs), F32),
        pltpu.VMEM((1, WIDE), F32),
        pltpu.VMEM((NDIR, 1, WIDE), F32),
        pltpu.VMEM((1, WIDE), F32),
        pltpu.VMEM((NCLS, 1, WIDE), F32),
    ]
    dma = pltpu.SemaphoreType.DMA
    sems = [dma((4,)), dma, dma, dma, dma, dma((NY,)), dma, dma((NX, NY))] + [dma] * 6
    out = pl.pallas_call(
        kernel,
        out_shape=jax.ShapeDtypeStruct((2, ROWS), F32),
        in_specs=[pl.BlockSpec(memory_space=pl.ANY)] * 5,
        out_specs=vmem,
        scratch_shapes=scratch + sems,
        compiler_params=pltpu.CompilerParams(
            collective_id=0, has_side_effects=True, vmem_limit_bytes=LIMIT
        ),
    )(
        particles,
        assignments.reshape(1, ROWS),
        defocus_bins.reshape(1, ROWS),
        ctf_table.T,
        references,
    )
    return out[0], out[1]


def solution(mesh):
    placed = (P("cls", "dir"), P("cls", None), P("cls"), P(), P("cls", "dir", None))
    return jax.shard_map(
        on_device, mesh=mesh, in_specs=placed, out_specs=(P("cls"), P("cls")), check_vma=False
    )
```

```python
import math

import jax
import jax.numpy as jnp
from jax import lax
from jax.experimental import pallas as pl
from jax.experimental.pallas import tpu as pltpu
from jax.sharding import PartitionSpec as P

CYCLES = 33
ANGLES = 64
ROTS = 16
WIDE = 2 * ANGLES
FEAT = CYCLES * WIDE
STEP = 2 * (ANGLES // ROTS)
SCALE = 1.0 / math.sqrt(FEAT / 3.0)
NCLS = 16
NX = 4
NY = 8
NDIR = NX * NY
ROWS = 16
CAP = 3
SLOTS = NCLS * CAP
BINS = 64
HALF = ROTS // 2
OUTWARD = (8, 9, 7, 10, 6, 11, 5, 12, 4, 13, 3, 14, 2, 15, 1)
TOTAL = 256
MESH = pl.DeviceIdType.MESH
HIGH = lax.Precision.HIGHEST
F32 = jnp.float32
BF16 = jnp.bfloat16
I32 = jnp.int32
LIMIT = 63 * 1024 * 1024


def iota(shape, dim):
    return lax.broadcasted_iota(I32, shape, dim)


def to_column(row, n):
    keep = iota((n, n), 0) == iota((n, n), 1)
    return jnp.sum(jnp.where(keep, jnp.broadcast_to(row, (n, n)), 0), axis=1, keepdims=True)


def to_row(column, n, lanes):
    keep = iota((n, lanes), 0) == iota((n, lanes), 1)
    return jnp.sum(
        jnp.where(keep, jnp.broadcast_to(column, (n, lanes)), 0), axis=0, keepdims=True
    )


def settle(ref, sem):
    pltpu.make_async_copy(ref, ref, sem).wait()


def kernel(
    part_hbm, assign_hbm, bins_hbm, table_hbm, refs_hbm, out_ref,
    part_ref, assign_ref, bins_ref, table_ref, tbuf, energy, bsend, brecv,
    grid, aux4, lhs, acc, dsend, dbuf, esend, ebuf,
    in_sem, load_sem, b_send, b_recv, y_send, y_recv, x_send, x_recv, u_send, u_recv,
    d_send, d_recv, e_send, e_recv,
):
    me_c = lax.axis_index("cls")
    me_d = lax.axis_index("dir")
    x = lax.rem(me_d, NX)
    y = lax.div(me_d, NX)

    barrier = pltpu.get_barrier_semaphore()
    peers = [(lax.rem(me_c + d, NCLS), me_d) for d in OUTWARD]
    peers += [(me_c, lax.rem(y + d, NY) * NX + x) for d in range(1, NY)]
    peers += [(me_c, y * NX + lax.rem(x + d, NX)) for d in range(1, NX)]
    for peer in peers:
        pl.semaphore_signal(barrier, inc=1, device_id=peer, device_id_type=MESH)
    inputs = [
        pltpu.make_async_copy(source, target, in_sem.at[n])
        for n, (source, target) in enumerate(
            [
                (assign_hbm, assign_ref),
                (bins_hbm, bins_ref),
                (table_hbm, table_ref),
                (part_hbm, part_ref),
            ]
        )
    ]
    for copy in inputs:
        copy.start()
    dirs = refs_hbm.shape[1]
    load = pltpu.make_async_copy(refs_hbm.at[0], tbuf.at[pl.ds(0, dirs)], load_sem)
    load.start()

    q = iota((4 * ROWS, TOTAL), 0)
    unpack = (iota((4 * ROWS, TOTAL), 1) == (q & 15) * ROWS + (q >> 4)).astype(F32).astype(BF16)
    for copy in inputs:
        copy.wait()

    assign_row = assign_ref[...]
    assign = to_column(assign_row, ROWS)
    bins = to_column(bins_ref[...], ROWS)
    together = assign == jnp.broadcast_to(assign_row, (ROWS, ROWS))
    down, across = iota((ROWS, ROWS), 0), iota((ROWS, ROWS), 1)
    placing = jnp.sum((together & (across < down)).astype(I32), axis=1, keepdims=True)
    placing_row = jnp.sum((together & (down < across)).astype(I32), axis=0, keepdims=True)

    at = iota((NCLS * ROWS, ROWS), 0)
    named = assign_row == at >> 4
    pack_main = (named & ((at & (ROWS - 1)) == placing_row)).astype(F32).astype(BF16)
    pack_aux = (named & ((at & (ROWS - 1)) == CAP)).astype(F32).astype(BF16)

    onehot = bins == iota((ROWS, BINS), 1)
    row_a = table_ref[pl.ds(me_d, 1), :]
    row_b = table_ref[pl.ds(me_d + 1, 1), :]
    ctf_a = jnp.sum(jnp.where(onehot, row_a, 0.0), axis=1, keepdims=True)
    ctf_b = jnp.sum(jnp.where(onehot, row_b, 0.0), axis=1, keepdims=True)
    raw = part_ref[...].astype(F32)
    wide = iota((ROWS, WIDE), 1)
    main = raw[:, :WIDE]
    main = main * jnp.where(wide < WIDE - 4 * me_d, ctf_a, ctf_b)
    main = pltpu.roll(main, 4 * me_d, 1)
    left = jnp.concatenate([raw[:, WIDE:], jnp.zeros((ROWS, WIDE - 4), F32)], axis=1) * ctf_b
    aux = jnp.where(wide == 96 + placing, (bins + 1).astype(F32), 0.0)
    for t in range(CAP):
        aux = aux + jnp.where(placing == t, pltpu.roll(left, 12 * y + 4 * t, 1), 0.0)
    bsend[...] = (
        jnp.dot(pack_main, main.astype(BF16), preferred_element_type=F32)
        + jnp.dot(pack_aux, aux.astype(BF16), preferred_element_type=F32)
    ).astype(BF16)
    mine = pl.ds(pl.multiple_of(me_c * ROWS, ROWS), ROWS)
    brecv[mine] = bsend[mine]

    pl.semaphore_wait(barrier, len(peers))

    for d in OUTWARD:
        to = lax.rem(me_c + d, NCLS)
        pltpu.make_async_remote_copy(
            src_ref=bsend.at[pl.ds(pl.multiple_of(to * ROWS, ROWS), ROWS)],
            dst_ref=brecv.at[mine], send_sem=b_send, recv_sem=b_recv,
            device_id=(to, me_d), device_id_type=MESH,
        ).start()

    load.wait()
    lanes = iota((1, WIDE), 1)
    total = jnp.zeros((dirs, WIDE), F32)
    for k in range(CYCLES):
        block = tbuf[:dirs, k * WIDE : (k + 1) * WIDE]
        tbuf[dirs:, k * WIDE : (k + 1) * WIDE] = pltpu.roll(block, WIDE // 2, 1)
        block = block.astype(F32)
        total = jnp.where(lanes == k, jnp.sum(block * block, axis=1, keepdims=True), total)
    energy[...] = total

    b_all = brecv.at[pl.ds(0, (NCLS - 1) * ROWS)]
    settle(b_all, b_recv)
    unpacked = jnp.dot(unpack, brecv[...], preferred_element_type=F32)
    own = grid.at[y, x]
    own[...] = unpacked.astype(BF16)

    def forward(rho):
        row = lax.rem(y + rho, NY)
        block = grid.at[row, x, pl.ds(0, SLOTS)]
        for d in (2, 1, 3):
            pltpu.make_async_remote_copy(
                src_ref=block, dst_ref=block, send_sem=x_send, recv_sem=x_recv.at[d, rho],
                device_id=(me_c, y * NX + lax.rem(x + d, NX)), device_id_type=MESH,
            ).start()

    for d in (1, 7, 2, 6, 3, 5, 4):
        pltpu.make_async_remote_copy(
            src_ref=own, dst_ref=own, send_sem=y_send, recv_sem=y_recv.at[NY - d],
            device_id=(me_c, lax.rem(y + d, NY) * NX + x), device_id_type=MESH,
        ).start()
    forward(0)

    nt = (((1,), (1,)), ((), ()))
    got = jnp.concatenate(
        [unpacked[SLOTS:, 96 + t : 97 + t] for t in range(CAP)], axis=0
    ).astype(I32)
    bin_hot = (got == iota((SLOTS, BINS), 1) + 1).astype(F32)
    table = jnp.concatenate([table_ref[...], jnp.zeros((WIDE - CYCLES, BINS), F32)], axis=0)
    ctf = lax.dot_general(bin_hot, table, nt, precision=HIGH, preferred_element_type=F32)
    penalty = 0.5 * lax.dot_general(
        energy[...], ctf * ctf, nt, precision=HIGH, preferred_element_type=F32
    )
    penalty = jnp.concatenate([penalty] * HALF, axis=1)

    for rho in (1, 7, 2, 6, 3, 5, 4):
        settle(grid.at[0, 0], y_recv.at[rho])
        forward(rho)
    over = jnp.zeros((ROWS, WIDE), F32)
    for row in range(NY):
        over = over + grid[row, x, SLOTS:, :].astype(F32)
    aux4[x] = over.astype(BF16)
    for d in (2, 1, 3):
        pltpu.make_async_remote_copy(
            src_ref=aux4.at[x], dst_ref=aux4.at[x], send_sem=u_send, recv_sem=u_recv,
            device_id=(me_c, y * NX + lax.rem(x + d, NX)), device_id_type=MESH,
        ).start()

    at = iota((1, CAP * WIDE), 1)
    place, at = at >> 7, at & (WIDE - 1)
    spread_to = ((at >> 2) & 3) * WIDE + (at >> 4) * 12 + place * 4 + (at & 3)
    spreading = (iota((NX * WIDE, CAP * WIDE), 0) == spread_to).astype(F32).astype(BF16)

    for rho in (0, 1, 7, 2, 6, 3, 5, 4):
        for d in range(1, NX):
            settle(grid.at[0, 0, pl.ds(0, SLOTS)], x_recv.at[d, rho])
    settle(aux4.at[pl.ds(0, 3)], u_recv)

    rest = jnp.concatenate([aux4[c] for c in range(NX)], axis=1)
    rest = jnp.dot(rest, spreading, preferred_element_type=F32).astype(BF16)
    rest = jnp.concatenate([rest[:, t * WIDE : (t + 1) * WIDE] for t in range(CAP)], axis=0)

    def turn(block, at):
        for r in range(HALF):
            lhs[r * SLOTS : (r + 1) * SLOTS, at * WIDE : (at + 1) * WIDE] = pltpu.roll(
                block, r * STEP, 1
            )

    def select(low, high):
        return ((lanes >= low) & (lanes < high)).astype(F32).astype(BF16)

    def cycle(k):
        block = None
        if k < NDIR:
            block = grid[k // NX, k % NX, :SLOTS, :] * select(4 * k, WIDE)
        if k > 0:
            j = k - 1
            early = grid[j // NX, j % NX, :SLOTS, :] * select(0, 4 * j)
            early = early + rest * select(4 * j, 4 * k)
            block = early if block is None else block + early
        return block

    for row in range(NY):
        for c in range(NX):
            turn(cycle(row * NX + c), c)
        term = lax.dot_general(
            tbuf[:, row * NX * WIDE : (row + 1) * NX * WIDE], lhs[...], nt,
            preferred_element_type=F32,
        )
        if row == 0:
            acc[...] = term
        else:
            acc[...] += term
    turn(cycle(NDIR), 0)
    cross = acc[...] + lax.dot_general(
        tbuf[:, NDIR * WIDE :], lhs[:, :WIDE], nt, preferred_element_type=F32
    )
    top = jnp.maximum(cross[:dirs], cross[dirs:]) - penalty
    local = jnp.max(top, axis=0, keepdims=True) * SCALE
    for r in (4, 2, 1):
        local = jnp.maximum(local[:, : r * SLOTS], local[:, r * SLOTS :])
    local = jnp.concatenate([local, jnp.zeros((1, WIDE - SLOTS), F32)], axis=1)

    dsend[...] = local
    dbuf[me_d] = local
    far = sorted(range(1, NDIR), key=lambda d: -min(d // NX, NY - d // NX))
    for d in far:
        pltpu.make_async_remote_copy(
            src_ref=dsend, dst_ref=dbuf.at[me_d], send_sem=d_send, recv_sem=d_recv,
            device_id=(me_c, lax.rem(me_d + d, NDIR)), device_id_type=MESH,
        ).start()
    d_all = dbuf.at[pl.ds(0, NDIR - 1)]
    settle(d_all, d_recv)
    group = jnp.max(dbuf[...], axis=0)

    squares = jnp.sum(group * group, axis=1, keepdims=True)
    answer = jnp.where(lanes == SLOTS, squares, group)
    esend[...] = answer
    ebuf[me_c] = answer
    for d in OUTWARD:
        pltpu.make_async_remote_copy(
            src_ref=esend, dst_ref=ebuf.at[me_c], send_sem=e_send, recv_sem=e_recv,
            device_id=(lax.rem(me_c + d, NCLS), me_d), device_id_type=MESH,
        ).start()
    settle(b_all, b_send)
    settle(grid.at[pl.ds(0, 7), 0], y_send)
    settle(grid.at[pl.ds(0, NY), pl.ds(0, 3), pl.ds(0, SLOTS)], x_send)
    settle(aux4.at[pl.ds(0, 3)], u_send)
    settle(d_all, d_send)

    e_all = ebuf.at[pl.ds(0, NCLS - 1)]
    settle(e_all, e_recv)
    spread = jnp.zeros((1, WIDE), F32)
    chosen = jnp.zeros((ROWS, WIDE), F32)
    for g in range(NCLS):
        spread = spread + ebuf[g]
        chosen = jnp.where(assign == g, ebuf[g], chosen)
    spread = jnp.sum(jnp.where(lanes == SLOTS, spread, 0.0), axis=1, keepdims=True)
    best = jnp.sum(
        jnp.where(wide == placing * ROWS + me_c, chosen, 0.0), axis=1, keepdims=True
    )
    best = to_row(best, ROWS, ROWS)
    out_ref[0:1, :] = best
    out_ref[1:2, :] = best / jnp.sqrt(spread / TOTAL + 1e-05)
    settle(e_all, e_send)


def on_device(particles, assignments, defocus_bins, ctf_table, references):
    dirs = references.shape[1]
    vmem = pl.BlockSpec(memory_space=pltpu.VMEM)
    scratch = [
        pltpu.VMEM((ROWS, FEAT // NDIR), BF16),
        pltpu.VMEM((1, ROWS), I32),
        pltpu.VMEM((1, ROWS), I32),
        pltpu.VMEM((CYCLES, BINS), F32),
        pltpu.VMEM((2 * dirs, FEAT), BF16),
        pltpu.VMEM((dirs, WIDE), F32),
        pltpu.VMEM((NCLS * ROWS, WIDE), BF16),
        pltpu.VMEM((NCLS * ROWS, WIDE), BF16),
        pltpu.VMEM((NY, NX, 4 * ROWS, WIDE), BF16),
        pltpu.VMEM((NX, ROWS, WIDE), BF16),
        pltpu.VMEM((HALF * SLOTS, NX * WIDE), BF16),
        pltpu.VMEM((2 * dirs, HALF * SLOTS), F32),
        pltpu.VMEM((1, WIDE), F32),
        pltpu.VMEM((NDIR, 1, WIDE), F32),
        pltpu.VMEM((1, WIDE), F32),
        pltpu.VMEM((NCLS, 1, WIDE), F32),
    ]
    dma = pltpu.SemaphoreType.DMA
    sems = [dma((4,)), dma, dma, dma, dma, dma((NY,)), dma, dma((NX, NY))] + [dma] * 6
    out = pl.pallas_call(
        kernel,
        out_shape=jax.ShapeDtypeStruct((2, ROWS), F32),
        in_specs=[pl.BlockSpec(memory_space=pl.ANY)] * 5,
        out_specs=vmem,
        scratch_shapes=scratch + sems,
        compiler_params=pltpu.CompilerParams(
            collective_id=0, has_side_effects=True, vmem_limit_bytes=LIMIT
        ),
    )(
        particles,
        assignments.reshape(1, ROWS),
        defocus_bins.reshape(1, ROWS),
        ctf_table.T,
        references,
    )
    return out[0], out[1]


def solution(mesh):
    placed = (P("cls", "dir"), P("cls", None), P("cls"), P(), P("cls", "dir", None))
    return jax.shard_map(
        on_device, mesh=mesh, in_specs=placed, out_specs=(P("cls"), P("cls")), check_vma=False
    )
```

```python
import math

import jax
import jax.numpy as jnp
from jax import lax
from jax.experimental import pallas as pl
from jax.experimental.pallas import tpu as pltpu
from jax.sharding import PartitionSpec as P

CYCLES = 33
ANGLES = 64
ROTS = 16
WIDE = 2 * ANGLES
FEAT = CYCLES * WIDE
STEP = 2 * (ANGLES // ROTS)
SCALE = 1.0 / math.sqrt(FEAT / 3.0)
NCLS = 16
NX = 4
NY = 8
NDIR = NX * NY
ROWS = 16
CAP = 3
SLOTS = NCLS * CAP
BINS = 64
HALF = ROTS // 2
OUTWARD = (8, 9, 7, 10, 6, 11, 5, 12, 4, 13, 3, 14, 2, 15, 1)
TOTAL = 256
MESH = pl.DeviceIdType.MESH
HIGH = lax.Precision.HIGHEST
F32 = jnp.float32
BF16 = jnp.bfloat16
I32 = jnp.int32
LIMIT = 63 * 1024 * 1024


def iota(shape, dim):
    return lax.broadcasted_iota(I32, shape, dim)


def to_column(row, n):
    keep = iota((n, n), 0) == iota((n, n), 1)
    return jnp.sum(jnp.where(keep, jnp.broadcast_to(row, (n, n)), 0), axis=1, keepdims=True)


def to_row(column, n, lanes):
    keep = iota((n, lanes), 0) == iota((n, lanes), 1)
    return jnp.sum(
        jnp.where(keep, jnp.broadcast_to(column, (n, lanes)), 0), axis=0, keepdims=True
    )


def settle(ref, sem):
    pltpu.make_async_copy(ref, ref, sem).wait()


def kernel(
    part_hbm, assign_hbm, bins_hbm, table_hbm, refs_hbm, out_ref,
    part_ref, assign_ref, bins_ref, table_ref, tbuf, energy, bsend, brecv,
    grid, aux4, lhs, acc, dsend, dbuf, esend, ebuf,
    in_sem, load_sem, b_send, b_recv, y_send, y_recv, x_send, x_recv, w_send, w_recv, u_send, u_recv,
    d_send, d_recv, e_send, e_recv,
):
    me_c = lax.axis_index("cls")
    me_d = lax.axis_index("dir")
    x = lax.rem(me_d, NX)
    y = lax.div(me_d, NX)

    barrier = pltpu.get_barrier_semaphore()
    peers = [(lax.rem(me_c + d, NCLS), me_d) for d in OUTWARD]
    peers += [(me_c, lax.rem(y + d, NY) * NX + x) for d in range(1, NY)]
    peers += [(me_c, y * NX + lax.rem(x + d, NX)) for d in range(1, NX)]
    for peer in peers:
        pl.semaphore_signal(barrier, inc=1, device_id=peer, device_id_type=MESH)
    inputs = [
        pltpu.make_async_copy(source, target, in_sem.at[n])
        for n, (source, target) in enumerate(
            [
                (assign_hbm, assign_ref),
                (bins_hbm, bins_ref),
                (table_hbm, table_ref),
                (part_hbm, part_ref),
            ]
        )
    ]
    for copy in inputs:
        copy.start()
    dirs = refs_hbm.shape[1]
    load = pltpu.make_async_copy(refs_hbm.at[0], tbuf.at[pl.ds(0, dirs)], load_sem)
    load.start()

    q = iota((4 * ROWS, TOTAL), 0)
    unpack = (iota((4 * ROWS, TOTAL), 1) == (q & 15) * ROWS + (q >> 4)).astype(F32).astype(BF16)
    for copy in inputs:
        copy.wait()

    assign_row = assign_ref[...]
    assign = to_column(assign_row, ROWS)
    bins = to_column(bins_ref[...], ROWS)
    together = assign == jnp.broadcast_to(assign_row, (ROWS, ROWS))
    down, across = iota((ROWS, ROWS), 0), iota((ROWS, ROWS), 1)
    placing = jnp.sum((together & (across < down)).astype(I32), axis=1, keepdims=True)
    placing_row = jnp.sum((together & (down < across)).astype(I32), axis=0, keepdims=True)

    at = iota((NCLS * ROWS, ROWS), 0)
    named = assign_row == at >> 4
    pack_main = (named & ((at & (ROWS - 1)) == placing_row)).astype(F32).astype(BF16)
    pack_aux = (named & ((at & (ROWS - 1)) == CAP)).astype(F32).astype(BF16)

    onehot = bins == iota((ROWS, BINS), 1)
    row_a = table_ref[pl.ds(me_d, 1), :]
    row_b = table_ref[pl.ds(me_d + 1, 1), :]
    ctf_a = jnp.sum(jnp.where(onehot, row_a, 0.0), axis=1, keepdims=True)
    ctf_b = jnp.sum(jnp.where(onehot, row_b, 0.0), axis=1, keepdims=True)
    raw = part_ref[...].astype(F32)
    wide = iota((ROWS, WIDE), 1)
    main = raw[:, :WIDE]
    main = main * jnp.where(wide < WIDE - 4 * me_d, ctf_a, ctf_b)
    main = pltpu.roll(main, 4 * me_d, 1)
    left = jnp.concatenate([raw[:, WIDE:], jnp.zeros((ROWS, WIDE - 4), F32)], axis=1) * ctf_b
    aux = jnp.where(wide == 96 + placing, (bins + 1).astype(F32), 0.0)
    for t in range(CAP):
        aux = aux + jnp.where(placing == t, pltpu.roll(left, 12 * y + 4 * t, 1), 0.0)
    bsend[...] = (
        jnp.dot(pack_main, main.astype(BF16), preferred_element_type=F32)
        + jnp.dot(pack_aux, aux.astype(BF16), preferred_element_type=F32)
    ).astype(BF16)
    mine = pl.ds(pl.multiple_of(me_c * ROWS, ROWS), ROWS)
    brecv[mine] = bsend[mine]

    pl.semaphore_wait(barrier, len(peers))

    for d in OUTWARD:
        to = lax.rem(me_c + d, NCLS)
        pltpu.make_async_remote_copy(
            src_ref=bsend.at[pl.ds(pl.multiple_of(to * ROWS, ROWS), ROWS)],
            dst_ref=brecv.at[mine], send_sem=b_send, recv_sem=b_recv,
            device_id=(to, me_d), device_id_type=MESH,
        ).start()

    load.wait()
    lanes = iota((1, WIDE), 1)
    total = jnp.zeros((dirs, WIDE), F32)
    for k in range(CYCLES):
        block = tbuf[:dirs, k * WIDE : (k + 1) * WIDE]
        tbuf[dirs:, k * WIDE : (k + 1) * WIDE] = pltpu.roll(block, WIDE // 2, 1)
        block = block.astype(F32)
        total = jnp.where(lanes == k, jnp.sum(block * block, axis=1, keepdims=True), total)
    energy[...] = total

    b_all = brecv.at[pl.ds(0, (NCLS - 1) * ROWS)]
    settle(b_all, b_recv)
    unpacked = jnp.dot(unpack, brecv[...], preferred_element_type=F32)
    grid[y, x] = unpacked.astype(BF16)
    own = grid.at[y, x, pl.ds(0, SLOTS)]
    own_aux = grid.at[y, x, pl.ds(SLOTS, ROWS)]

    def forward(rho):
        row = lax.rem(y + rho, NY)
        block = grid.at[row, x, pl.ds(0, SLOTS)]
        for d in (2, 1, 3):
            pltpu.make_async_remote_copy(
                src_ref=block, dst_ref=block, send_sem=x_send, recv_sem=x_recv.at[d, rho],
                device_id=(me_c, y * NX + lax.rem(x + d, NX)), device_id_type=MESH,
            ).start()

    for d in (4, 3, 5, 2, 6, 1, 7):
        pltpu.make_async_remote_copy(
            src_ref=own_aux, dst_ref=own_aux, send_sem=w_send, recv_sem=w_recv,
            device_id=(me_c, lax.rem(y + d, NY) * NX + x), device_id_type=MESH,
        ).start()
    for d in (1, 7, 2, 6, 3, 5, 4):
        pltpu.make_async_remote_copy(
            src_ref=own, dst_ref=own, send_sem=y_send, recv_sem=y_recv.at[NY - d],
            device_id=(me_c, lax.rem(y + d, NY) * NX + x), device_id_type=MESH,
        ).start()
    forward(0)

    nt = (((1,), (1,)), ((), ()))
    got = jnp.concatenate(
        [unpacked[SLOTS:, 96 + t : 97 + t] for t in range(CAP)], axis=0
    ).astype(I32)
    bin_hot = (got == iota((SLOTS, BINS), 1) + 1).astype(F32)
    table = jnp.concatenate([table_ref[...], jnp.zeros((WIDE - CYCLES, BINS), F32)], axis=0)
    ctf = lax.dot_general(bin_hot, table, nt, precision=HIGH, preferred_element_type=F32)
    penalty = 0.5 * lax.dot_general(
        energy[...], ctf * ctf, nt, precision=HIGH, preferred_element_type=F32
    )
    penalty = jnp.concatenate([penalty] * HALF, axis=1)

    def pass_on(rows):
        for rho in rows:
            settle(own, y_recv.at[rho])
            forward(rho)

    pass_on((1, 7))
    settle(grid.at[pl.ds(0, 7), 0, pl.ds(0, ROWS)], w_recv)
    over = jnp.zeros((ROWS, WIDE), F32)
    for row in range(NY):
        over = over + grid[row, x, SLOTS:, :].astype(F32)
    aux4[x] = over.astype(BF16)
    for d in (2, 1, 3):
        pltpu.make_async_remote_copy(
            src_ref=aux4.at[x], dst_ref=aux4.at[x], send_sem=u_send, recv_sem=u_recv,
            device_id=(me_c, y * NX + lax.rem(x + d, NX)), device_id_type=MESH,
        ).start()

    pass_on((2, 6, 3, 5, 4))

    at = iota((1, CAP * WIDE), 1)
    place, at = at >> 7, at & (WIDE - 1)
    spread_to = ((at >> 2) & 3) * WIDE + (at >> 4) * 12 + place * 4 + (at & 3)
    spreading = (iota((NX * WIDE, CAP * WIDE), 0) == spread_to).astype(F32).astype(BF16)

    settle(aux4.at[pl.ds(0, 3)], u_recv)

    rest = jnp.concatenate([aux4[c] for c in range(NX)], axis=1)
    rest = jnp.dot(rest, spreading, preferred_element_type=F32).astype(BF16)
    rest = jnp.concatenate([rest[:, t * WIDE : (t + 1) * WIDE] for t in range(CAP)], axis=0)

    def turn(block, at):
        for r in range(HALF):
            lhs[r * SLOTS : (r + 1) * SLOTS, at * WIDE : (at + 1) * WIDE] = pltpu.roll(
                block, r * STEP, 1
            )

    def select(low, high):
        return ((lanes >= low) & (lanes < high)).astype(F32).astype(BF16)

    def early(row, c, j):
        return grid[row, c, :SLOTS, :] * select(0, 4 * j) + rest * select(4 * j, 4 * j + 4)

    def add_row(rho):
        row = lax.rem(y + rho, NY)
        for c in range(NX):
            k = row * NX + c
            before = (row, c - 1) if c else (lax.rem(row + NY - 1, NY), NX - 1)
            turn(grid[row, c, :SLOTS, :] * select(4 * k, WIDE) + early(*before, k - 1), c)
        term = lax.dot_general(
            tbuf[:, pl.ds(pl.multiple_of(row * NX * WIDE, NX * WIDE), NX * WIDE)], lhs[...], nt,
            preferred_element_type=F32,
        )
        if rho == 0:
            acc[...] = term
        else:
            acc[...] += term

    for rho, ready in (
        (0, ()), (7, (0,)), (1, (1,)), (6, (7,)), (2, (2,)), (5, (6,)), (3, (3,)), (4, (4, 5))
    ):
        for d in range(1, NX):
            settle(grid.at[0, 0, pl.ds(0, SLOTS)], x_recv.at[d, rho])
        for r in ready:
            add_row(r)
    turn(early(NY - 1, NX - 1, NDIR - 1), 0)
    cross = acc[...] + lax.dot_general(
        tbuf[:, NDIR * WIDE :], lhs[:, :WIDE], nt, preferred_element_type=F32
    )
    top = jnp.maximum(cross[:dirs], cross[dirs:]) - penalty
    local = jnp.max(top, axis=0, keepdims=True) * SCALE
    for r in (4, 2, 1):
        local = jnp.maximum(local[:, : r * SLOTS], local[:, r * SLOTS :])
    local = jnp.concatenate([local, jnp.zeros((1, WIDE - SLOTS), F32)], axis=1)

    dsend[...] = local
    dbuf[me_d] = local
    far = sorted(range(1, NDIR), key=lambda d: -min(d // NX, NY - d // NX))
    for d in far:
        pltpu.make_async_remote_copy(
            src_ref=dsend, dst_ref=dbuf.at[me_d], send_sem=d_send, recv_sem=d_recv,
            device_id=(me_c, lax.rem(me_d + d, NDIR)), device_id_type=MESH,
        ).start()
    d_all = dbuf.at[pl.ds(0, NDIR - 1)]
    settle(d_all, d_recv)
    group = jnp.max(dbuf[...], axis=0)

    squares = jnp.sum(group * group, axis=1, keepdims=True)
    answer = jnp.where(lanes == SLOTS, squares, group)
    esend[...] = answer
    ebuf[me_c] = answer
    for d in OUTWARD:
        pltpu.make_async_remote_copy(
            src_ref=esend, dst_ref=ebuf.at[me_c], send_sem=e_send, recv_sem=e_recv,
            device_id=(lax.rem(me_c + d, NCLS), me_d), device_id_type=MESH,
        ).start()
    settle(b_all, b_send)
    settle(grid.at[pl.ds(0, 7), 0, pl.ds(0, SLOTS)], y_send)
    settle(grid.at[pl.ds(0, 7), 0, pl.ds(0, ROWS)], w_send)
    settle(grid.at[pl.ds(0, NY), pl.ds(0, 3), pl.ds(0, SLOTS)], x_send)
    settle(aux4.at[pl.ds(0, 3)], u_send)
    settle(d_all, d_send)

    e_all = ebuf.at[pl.ds(0, NCLS - 1)]
    settle(e_all, e_recv)
    spread = jnp.zeros((1, WIDE), F32)
    chosen = jnp.zeros((ROWS, WIDE), F32)
    for g in range(NCLS):
        spread = spread + ebuf[g]
        chosen = jnp.where(assign == g, ebuf[g], chosen)
    spread = jnp.sum(jnp.where(lanes == SLOTS, spread, 0.0), axis=1, keepdims=True)
    best = jnp.sum(
        jnp.where(wide == placing * ROWS + me_c, chosen, 0.0), axis=1, keepdims=True
    )
    best = to_row(best, ROWS, ROWS)
    out_ref[0:1, :] = best
    out_ref[1:2, :] = best / jnp.sqrt(spread / TOTAL + 1e-05)
    settle(e_all, e_send)


def on_device(particles, assignments, defocus_bins, ctf_table, references):
    dirs = references.shape[1]
    vmem = pl.BlockSpec(memory_space=pltpu.VMEM)
    scratch = [
        pltpu.VMEM((ROWS, FEAT // NDIR), BF16),
        pltpu.VMEM((1, ROWS), I32),
        pltpu.VMEM((1, ROWS), I32),
        pltpu.VMEM((CYCLES, BINS), F32),
        pltpu.VMEM((2 * dirs, FEAT), BF16),
        pltpu.VMEM((dirs, WIDE), F32),
        pltpu.VMEM((NCLS * ROWS, WIDE), BF16),
        pltpu.VMEM((NCLS * ROWS, WIDE), BF16),
        pltpu.VMEM((NY, NX, 4 * ROWS, WIDE), BF16),
        pltpu.VMEM((NX, ROWS, WIDE), BF16),
        pltpu.VMEM((HALF * SLOTS, NX * WIDE), BF16),
        pltpu.VMEM((2 * dirs, HALF * SLOTS), F32),
        pltpu.VMEM((1, WIDE), F32),
        pltpu.VMEM((NDIR, 1, WIDE), F32),
        pltpu.VMEM((1, WIDE), F32),
        pltpu.VMEM((NCLS, 1, WIDE), F32),
    ]
    dma = pltpu.SemaphoreType.DMA
    sems = [dma((4,)), dma, dma, dma, dma, dma((NY,)), dma, dma((NX, NY))] + [dma] * 8
    out = pl.pallas_call(
        kernel,
        out_shape=jax.ShapeDtypeStruct((2, ROWS), F32),
        in_specs=[pl.BlockSpec(memory_space=pl.ANY)] * 5,
        out_specs=vmem,
        scratch_shapes=scratch + sems,
        compiler_params=pltpu.CompilerParams(
            collective_id=0, has_side_effects=True, vmem_limit_bytes=LIMIT
        ),
    )(
        particles,
        assignments.reshape(1, ROWS),
        defocus_bins.reshape(1, ROWS),
        ctf_table.T,
        references,
    )
    return out[0], out[1]


def solution(mesh):
    placed = (P("cls", "dir"), P("cls", None), P("cls"), P(), P("cls", "dir", None))
    return jax.shard_map(
        on_device, mesh=mesh, in_specs=placed, out_specs=(P("cls"), P("cls")), check_vma=False
    )
```
